512 devices in a mesh: layer: 16 (over y, z_hi, core), row: 4 (over x), col: 8 (over z_lo).
Axes of the slice: x: 4, y: 4, z: 16 (z_hi: 2, z_lo: 8; z = z_hi * 8 + z_lo), core: 2. Of those that a mesh axis runs over, the one named last changes fastest.
Arguments:
- front: float32 [16, 4096, 4096], P('layer', 'row', 'col'), may hold values from -0.875 to 0.875
- inverses: float32 [16, 2, 512, 512], P('layer', None, 'row')
- pattern: int32 [2, 32, 32], replicated, may hold values 0 or 1
- order: int32 [8], replicated, may hold values from 0 to 7, each once
- lists: int32 [16, 32, 32], P('layer'), may hold values from 0 to 15
Outputs:
- ancestor: float32 [16, 4096, 4096], P('layer', 'row', 'col')
The draws below stay inside these ranges and needn't reach their ends.
Inputs may be any that keep to these rules, and one draw needn't show every extreme that they name: `order`: every panel appears once.
All inputs are finite; a program needn't handle non-finite values.
Results may differ from the reference program's by a relative error of at most 0.00022.
Values sent between devices are 32-bit elements; how exact they have to be, the bound alone decides.
No kernel may reach another device: no remote copies, remote signals or barrier semaphores. Data moves between devices by JAX's collectives and lax.ppermute only.
A program may use at most 64 MiB of HBM per device.

```python
import math
import jax
import jax.numpy as jnp
from jax import lax

F = 4096
P_SIZE = 512
BLK = 128
SECTIONS = 2
LAYERS = 16
LEVELS = 4
NB = 32
NPANEL = 8


def draw_inverses(key, part):
    key = jax.random.fold_in(key, 11)
    first_key, second_key = jax.random.split(key)
    scattered = jax.random.truncated_normal(first_key, -4.0, 4.0, (LAYERS, SECTIONS, P_SIZE, P_SIZE), jnp.float32) * (0.5 / math.sqrt(P_SIZE))
    diagonal = jnp.exp(jax.random.uniform(second_key, (LAYERS, SECTIONS, P_SIZE), jnp.float32, math.log(0.5), math.log(2.0)))
    identity = (jnp.arange(P_SIZE)[:, None] == jnp.arange(P_SIZE)[None, :]).astype(jnp.float32)
    return scattered + identity * diagonal[:, :, :, None]


def with_ends(drawn, stream_key, low, high):
    longest = drawn.shape.index(max(drawn.shape))
    spots = []
    for shift in (0, 1):
        where = [jax.random.randint(jax.random.fold_in(stream_key, axis), (), 0, length) for axis, length in enumerate(drawn.shape)]
        where[longest] = (where[longest] + shift) % drawn.shape[longest]
        spots.append(tuple(where))
    return drawn.at[spots[0]].set(low).at[spots[1]].set(high)


def block_scale(key, dims, pieces, least, top_value):
    loudness, own = 1.0, jax.random.fold_in(key, 6)
    for dim, parts in pieces:
        draws = jnp.exp(jax.random.uniform(jax.random.fold_in(own, dim), (parts,), jnp.float32, least / len(pieces), top_value / len(pieces)))
        loudness = loudness * jnp.repeat(draws, dims[dim] // parts).reshape([-1 if axis == dim else 1 for axis in range(len(dims))])
    return loudness


def normal_values(key, shape, spread, most, cuts=(), held_as=jnp.bfloat16):
    drawn = spread * jax.random.normal(key, shape, jnp.float32)
    if cuts:
        drawn = drawn * block_scale(key, shape, cuts, -0.22, 0.18)
    return jnp.clip(drawn, -most, most).astype(held_as)


def setup_inputs(seed: int = 0) -> dict:
    streams_of = jax.random.split(jax.random.key(seed), 6)
    front = normal_values(streams_of[0], (LAYERS, F, F), 0.15, 0.875, ((0, 16), (1, 4), (2, 8)), jnp.float32)
    inverses = draw_inverses(jax.random.fold_in(streams_of[5], 71), 0)
    pattern = with_ends((jax.random.randint(streams_of[2], (SECTIONS, NB, NB), 0, 3) < 2).astype(jnp.int32), jax.random.fold_in(streams_of[2], 1), 0, 1)
    order = jax.random.permutation(streams_of[3], NPANEL).astype(jnp.int32)
    lists = with_ends(jax.random.randint(streams_of[4], (LAYERS, NB, NB), 0, LAYERS), jax.random.fold_in(streams_of[4], 1), 0, LAYERS - 1).astype(jnp.int32)
    return dict(front=front, inverses=inverses, pattern=pattern, order=order, lists=lists)


EXACT_PRECISION = lax.Precision.HIGHEST


def eliminate(matrix, inverse_all, order, pattern):
    block_count = F // BLK
    panel_numbers = jnp.arange(F // P_SIZE)
    eliminated = jnp.zeros((F // P_SIZE,), jnp.float32)
    for section_index in range(SECTIONS):
        target = order[section_index]
        first_index = (target * P_SIZE).astype(jnp.int32)
        eliminated = eliminated + (panel_numbers == target).astype(jnp.float32)
        alive_blocks = jnp.repeat(1.0 - eliminated, P_SIZE // BLK)
        pivot_row = lax.dynamic_slice_in_dim(matrix, first_index, P_SIZE, 0)
        pivot_col = lax.dynamic_slice_in_dim(matrix, first_index, P_SIZE, 1)
        scaled = jnp.dot(inverse_all[section_index], pivot_row, precision=EXACT_PRECISION, preferred_element_type=jnp.float32)
        update = jnp.dot(pivot_col, scaled, precision=EXACT_PRECISION, preferred_element_type=jnp.float32)
        update_mask = pattern[section_index].astype(jnp.float32) * alive_blocks[:, None] * alive_blocks[None, :]
        blocked = matrix.reshape(block_count, BLK, block_count, BLK) - update.reshape(block_count, BLK, block_count, BLK) * update_mask[:, None, :, None]
        matrix = blocked.reshape(F, F)
    alive_blocks = jnp.repeat(1.0 - eliminated, P_SIZE // BLK)
    keep_mask = alive_blocks[:, None] * alive_blocks[None, :]
    return (matrix.reshape(block_count, BLK, block_count, BLK) * keep_mask[:, None, :, None]).reshape(F, F)


def reference(front, inverses, pattern, order, lists):
    accumulated = lax.map(lambda layer_pair: eliminate(layer_pair[0], layer_pair[1], order, pattern), (front, inverses))
    block_count = F // BLK
    for level_bit in range(LEVELS):
        distance = 2 ** level_bit
        partner = accumulated.reshape(LAYERS // (2 * distance), 2, distance, F, F)[:, ::-1].reshape(LAYERS, F, F)
        weights = ((lists // distance) % 2).astype(jnp.float32)
        summed = accumulated.reshape(LAYERS, block_count, BLK, block_count, BLK) + partner.reshape(LAYERS, block_count, BLK, block_count, BLK) * weights[:, :, None, :, None]
        accumulated = summed.reshape(LAYERS, F, F)
    return accumulated
```

```python
import jax
import jax.numpy as jnp
from jax import lax
from jax.sharding import PartitionSpec as P

F = 4096
P_SIZE = 512
BLK = 128
PB = P_SIZE // BLK


def matmul(left_side, right_side):
    return jnp.dot(
        left_side,
        right_side,
        precision=lax.Precision.HIGH,
        preferred_element_type=jnp.float32,
    )


def xor_send(value, axis, mask):
    pairs = [(source, source ^ mask) for source in range(lax.axis_size(axis))]
    return lax.ppermute(value, axis, pairs)


def pick(parts, index):
    out = parts[0]
    for k in range(1, len(parts)):
        out = jnp.where(index == k, parts[k], out)
    return out


def by_blocks(value, weights):
    rows, cols = value.shape
    wide = jnp.repeat(weights, BLK, axis=1)
    return (value.reshape(rows // BLK, BLK, cols) * wide[:, None, :]).reshape(rows, cols)


def gather_row(part, row):
    got = [part] + [xor_send(part, "row", k) for k in (1, 2, 3)]
    return [pick(got, row ^ q) for q in range(4)]


def body(front, inverses, pattern, order, lists):
    matrix = front[0]
    rows, cols = matrix.shape
    row = lax.axis_index("row")
    col = lax.axis_index("col")
    layer = lax.axis_index("layer")
    q0, q1 = order[0], order[1]
    rb, cb = rows // BLK, cols // BLK
    row_first, col_first = row * rb, col * cb
    half = rows // 2
    quarter = cols // 4

    every_list = lax.all_gather(lists[0], "layer", axis=0)

    h1 = q1 % 2
    own_first = lax.dynamic_slice_in_dim(matrix, h1 * half, half, 0)
    own_rest = lax.dynamic_slice_in_dim(matrix, (1 - h1) * half, half, 0)
    first = lax.psum(jnp.where(col == q0, own_first, 0.0), "col")
    rest = lax.psum(jnp.where(col == q0, own_rest, 0.0), "col")
    c1 = lax.psum(jnp.where(col == q1, matrix, 0.0), "col")

    inv_parts = gather_row(inverses[0], row)
    inv = jnp.concatenate(inv_parts, axis=1)
    cand = jnp.stack(
        [
            lax.dynamic_slice_in_dim(matrix, (q0 % 2) * half, half, 0),
            lax.dynamic_slice_in_dim(matrix, (q1 % 2) * half, half, 0),
        ]
    )

    def quarter_of(value, q):
        return lax.dynamic_slice_in_dim(value, q * quarter, quarter, 2)

    got = [quarter_of(cand, row)] + [
        xor_send(quarter_of(cand, row ^ k), "row", k) for k in (1, 2, 3)
    ]
    r0 = pick([g[0] for g in got], row ^ (q0 // 2))
    r1 = pick([g[1] for g in got], row ^ (q1 // 2))

    s0q = matmul(inv[0], r0)
    s0 = jnp.concatenate(gather_row(s0q, row), axis=1)
    s0xq = lax.psum(jnp.where(col == q1, s0q, 0.0), "col")
    s0x = jnp.concatenate(gather_row(s0xq, row), axis=1)

    panels = jnp.arange(F // P_SIZE)
    alive0 = (panels != q0).astype(jnp.float32)
    alive1 = alive0 * (panels != q1).astype(jnp.float32)
    a0 = jnp.repeat(alive0, PB)
    a1 = jnp.repeat(alive1, PB)
    full0 = pattern[0].astype(jnp.float32) * a0[:, None] * a0[None, :]
    full1 = pattern[1].astype(jnp.float32) * a1[:, None] * a1[None, :]
    keep = a1[:, None] * a1[None, :]

    def block(mask, at, shape):
        return lax.dynamic_slice(mask, at, shape)

    here = ((row_first, col_first), (rb, cb))
    mask0 = block(full0, *here)
    mask1 = block(full1, *here)
    kept = block(keep, *here)
    mask_c = block(full0, (row_first, q1 * PB), (rb, PB))
    mask_r = block(full0, (q1 * PB, col_first), (PB, cb))
    mask_rq = lax.dynamic_slice_in_dim(mask_r, row, 1, 1)

    y_got = [first] + [xor_send(first, "row", k) for k in (1, 2, 3)]
    y = pick(y_got, row ^ (q1 // 2))
    r1 = r1 - by_blocks(matmul(y, s0_quarter(s0, row, quarter)), mask_rq)
    s1q = matmul(inv[1], r1)
    s1 = jnp.concatenate(gather_row(s1q, row), axis=1)

    l0 = jnp.where(
        h1 == 0,
        jnp.concatenate([first, rest], axis=0),
        jnp.concatenate([rest, first], axis=0),
    )
    l1 = c1 - by_blocks(matmul(l0, s0x), mask_c)
    acc = by_blocks(
        matrix - by_blocks(matmul(l0, s0), mask0) - by_blocks(matmul(l1, s1), mask1), kept
    )

    mine = block(lists[0], *here)

    def bit(values, b):
        return (values // 2**b % 2).astype(jnp.float32)

    acc = acc + by_blocks(xor_send(acc, "layer", 1), bit(mine, 0))

    yy = layer // 4
    qrows = rows // 4
    qb = rb // 4
    quarters = acc.reshape(4, qrows, cols)

    def own(q):
        return lax.dynamic_index_in_dim(quarters, q, 0, keepdims=False)

    held = [own(yy)] + [xor_send(own(yy ^ k), "layer", 4 * k) for k in (1, 2, 3)]
    w = [
        lax.dynamic_slice(
            every_list, (layer ^ (4 * k), row_first + yy * qb, col_first), (1, qb, cb)
        )[0]
        for k in range(4)
    ]
    for k in range(4):
        other = xor_send(held[k], "layer", 2)
        held[k] = held[k] + by_blocks(other, bit(w[k], 1))
    for b in (2, 3):
        d = b - 1
        held = [held[k] + by_blocks(held[k ^ d], bit(w[k], b)) for k in range(4)]
    back = [held[0]] + [xor_send(held[k], "layer", 4 * k) for k in (1, 2, 3)]
    out = jnp.zeros((4, qrows, cols), jnp.float32)
    for k in range(4):
        out = lax.dynamic_update_index_in_dim(out, back[k], yy ^ k, 0)
    return out.reshape(1, rows, cols)


def s0_quarter(s0, row, quarter):
    return lax.dynamic_slice_in_dim(s0, row * quarter, quarter, 1)


def solution(mesh):
    placed = (
        P("layer", "row", "col"),
        P("layer", None, "row", None),
        P(),
        P(),
        P("layer", None, None),
    )
    return jax.shard_map(
        body, mesh=mesh, in_specs=placed, out_specs=P("layer", "row", "col"), check_vma=False
    )
```

```python
import functools

import jax
import jax.numpy as jnp
from jax import lax
from jax.experimental import pallas as pl
from jax.experimental.pallas import tpu as pltpu
from jax.sharding import PartitionSpec as P

F = 4096
P_SIZE = 512
BLK = 128
PB = P_SIZE // BLK
STEP = 2


def matmul(left_side, right_side):
    return jnp.dot(
        left_side,
        right_side,
        precision=lax.Precision.HIGH,
        preferred_element_type=jnp.float32,
    )


def xor_send(value, axis, mask):
    pairs = [(source, source ^ mask) for source in range(lax.axis_size(axis))]
    return lax.ppermute(value, axis, pairs)


def pick(parts, index):
    out = parts[0]
    for k in range(1, len(parts)):
        out = jnp.where(index == k, parts[k], out)
    return out


def by_blocks(value, weights):
    rows, cols = value.shape
    wide = jnp.repeat(weights, BLK, axis=1)
    return (value.reshape(rows // BLK, BLK, cols) * wide[:, None, :]).reshape(rows, cols)


def gather_row(part, row):
    got = [part] + [xor_send(part, "row", k) for k in (1, 2, 3)]
    return [pick(got, row ^ q) for q in range(4)]


def exchange_row(candidate, row, source):
    quarter = candidate.shape[1] // 4

    def part(q):
        return lax.dynamic_slice_in_dim(candidate, q * quarter, quarter, 1)

    got = [part(row)] + [xor_send(part(row ^ k), "row", k) for k in (1, 2, 3)]
    return pick(got, row ^ source)


def spread(panel, col, source):
    count = lax.axis_size("col")
    share = panel.shape[0] // count

    def branch(origin, value):
        def part(t):
            return value[t * share : (t + 1) * share]

        order = sorted((t for t in range(count) if t != origin), key=lambda t: -abs(t - origin))
        total = jnp.where(col == origin, part(origin), 0.0)
        for t in order:
            total = jnp.where(col == t, lax.ppermute(part(t), "col", [(origin, t)]), total)
        return total

    return lax.switch(source, [functools.partial(branch, p) for p in range(count)], panel)


def blocks_of(rows, cols):
    return [(i, j) for i in range(rows // BLK) for j in range(cols // BLK)]


def pack_kernel(slots, value, packed):
    for b, (i, j) in enumerate(blocks_of(*value.shape)):
        slot = slots[b]

        @pl.when(slot >= 0)
        def _():
            packed[slot] = value[i * BLK : (i + 1) * BLK, j * BLK : (j + 1) * BLK]


def add_kernel(slots, value, packed, out):
    for b, (i, j) in enumerate(blocks_of(*value.shape)):
        slot = slots[b]
        at = (slice(i * BLK, (i + 1) * BLK), slice(j * BLK, (j + 1) * BLK))

        @pl.when(slot >= 0)
        def _():
            out[at] = value[at] + packed[slot]

        @pl.when(slot < 0)
        def _():
            out[at] = value[at]


SMEM = pl.BlockSpec(memory_space=pltpu.SMEM)
VMEM = pl.BlockSpec(memory_space=pltpu.VMEM)
PARAMS = pltpu.CompilerParams(vmem_limit_bytes=24 * 2**20)


def pack(slots, value, size):
    return pl.pallas_call(
        pack_kernel,
        out_shape=jax.ShapeDtypeStruct((size, BLK, BLK), jnp.float32),
        in_specs=[SMEM, VMEM],
        out_specs=VMEM,
        compiler_params=PARAMS,
    )(slots, value)


def add_packed(slots, value, packed):
    return pl.pallas_call(
        add_kernel,
        out_shape=jax.ShapeDtypeStruct(value.shape, jnp.float32),
        in_specs=[SMEM, VMEM, VMEM],
        out_specs=VMEM,
        compiler_params=PARAMS,
    )(slots, value, packed)


def slots_of(wanted):
    flat = wanted.reshape(-1).astype(jnp.int32)
    return jnp.where(flat > 0, jnp.cumsum(flat) - 1, -1), jnp.sum(flat)


def listed_exchange(acc, wanted_here, wanted_there, mask):
    to_send, n_send = slots_of(wanted_there)
    to_add, n_add = slots_of(wanted_here)
    most = to_send.shape[0]

    def branch(size, value):
        packed = pack(to_send, value, size)
        return add_packed(to_add, value, xor_send(packed, "layer", mask))

    choices = [lambda value: value]
    choices += [functools.partial(branch, s) for s in range(STEP, most + 1, STEP)]
    return lax.switch((jnp.maximum(n_send, n_add) + STEP - 1) // STEP, choices, acc)


def body(front, inverses, pattern, order, lists):
    matrix = front[0]
    rows, cols = matrix.shape
    row = lax.axis_index("row")
    col = lax.axis_index("col")
    layer = lax.axis_index("layer")
    q0, q1 = order[0], order[1]
    rb, cb = rows // BLK, cols // BLK
    row_first, col_first = row * rb, col * cb
    half = rows // 2
    quarter = cols // 4

    panels = jnp.arange(F // P_SIZE)
    alive0 = (panels != q0).astype(jnp.float32)
    alive1 = alive0 * (panels != q1).astype(jnp.float32)
    a0 = jnp.repeat(alive0, PB)
    a1 = jnp.repeat(alive1, PB)
    here = ((row_first, col_first), (rb, cb))
    mask0 = lax.dynamic_slice(pattern[0].astype(jnp.float32) * a0[:, None] * a0[None, :], *here)
    mask1 = lax.dynamic_slice(pattern[1].astype(jnp.float32) * a1[:, None] * a1[None, :], *here)
    kept = lax.dynamic_slice(a1[:, None] * a1[None, :], *here)

    share = spread(matrix, col, q0)
    share, inverse_part, matrix, mine = lax.optimization_barrier(
        (share, inverses[0], matrix, lists[0])
    )
    left = lax.all_gather(share, "col", axis=0, tiled=True)
    mine = lax.dynamic_slice(mine, *here)
    theirs = xor_send(mine, "layer", 2)
    listed = [mine] + [xor_send(mine, "layer", 4 * k) for k in (1, 2, 3)]
    inv = jnp.concatenate(gather_row(inverse_part, row), axis=1)
    candidate = lax.dynamic_slice_in_dim(matrix, (q0 % 2) * half, half, 0)
    scaled = matmul(inv[0], exchange_row(candidate, row, q0 // 2))
    right = jnp.concatenate(gather_row(scaled, row), axis=1)
    matrix = matrix - by_blocks(matmul(left, right), mask0)

    share = spread(matrix, col, q1)
    share, matrix = lax.optimization_barrier((share, matrix))
    left = lax.all_gather(share, "col", axis=0, tiled=True)
    candidate = lax.dynamic_slice_in_dim(matrix, (q1 % 2) * half, half, 0)
    scaled = matmul(inv[1], exchange_row(candidate, row, q1 // 2))
    right = jnp.concatenate(gather_row(scaled, row), axis=1)
    acc = by_blocks(matrix - by_blocks(matmul(left, right), mask1), kept)

    def bit(values, b):
        return (values // 2**b % 2).astype(jnp.float32)

    acc = acc + by_blocks(xor_send(acc, "layer", 1), bit(mine, 0))

    acc = listed_exchange(acc, bit(mine, 1) * kept > 0, bit(theirs, 1) * kept > 0, 2)

    yy = layer // 4
    qrows = rows // 4
    qb = rb // 4
    quarters = acc.reshape(4, qrows, cols)

    def own(q):
        return lax.dynamic_index_in_dim(quarters, q, 0, keepdims=False)

    held = [own(yy)] + [xor_send(own(yy ^ k), "layer", 4 * k) for k in (1, 2, 3)]
    w = [lax.dynamic_slice_in_dim(values, yy * qb, qb, 0) for values in listed]
    for b in (2, 3):
        d = b - 1
        held = [held[k] + by_blocks(held[k ^ d], bit(w[k], b)) for k in range(4)]
    back = [held[0]] + [xor_send(held[k], "layer", 4 * k) for k in (1, 2, 3)]
    out = jnp.zeros((4, qrows, cols), jnp.float32)
    for k in range(4):
        out = lax.dynamic_update_index_in_dim(out, back[k], yy ^ k, 0)
    return out.reshape(1, rows, cols)


def solution(mesh):
    placed = (
        P("layer", "row", "col"),
        P("layer", None, "row", None),
        P(),
        P(),
        P("layer", None, None),
    )
    return jax.shard_map(
        body, mesh=mesh, in_specs=placed, out_specs=P("layer", "row", "col"), check_vma=False
    )
```

```python
import functools

import jax
import jax.numpy as jnp
from jax import lax
from jax.experimental import pallas as pl
from jax.experimental.pallas import tpu as pltpu
from jax.sharding import PartitionSpec as P

F = 4096
P_SIZE = 512
BLK = 128
PB = P_SIZE // BLK
STEP = 2


def matmul(left_side, right_side):
    return jnp.dot(
        left_side,
        right_side,
        precision=lax.Precision.HIGH,
        preferred_element_type=jnp.float32,
    )


def xor_send(value, axis, mask):
    pairs = [(source, source ^ mask) for source in range(lax.axis_size(axis))]
    return lax.ppermute(value, axis, pairs)


def pick(parts, index):
    out = parts[0]
    for k in range(1, len(parts)):
        out = jnp.where(index == k, parts[k], out)
    return out


def by_blocks(value, weights):
    rows, cols = value.shape
    wide = jnp.repeat(weights, BLK, axis=1)
    return (value.reshape(rows // BLK, BLK, cols) * wide[:, None, :]).reshape(rows, cols)


def gather_row(part, row):
    got = [part] + [xor_send(part, "row", k) for k in (1, 2, 3)]
    return [pick(got, row ^ q) for q in range(4)]


def exchange_row(candidate, row, source):
    quarter = candidate.shape[1] // 4

    def part(q):
        return lax.dynamic_slice_in_dim(candidate, q * quarter, quarter, 1)

    got = [part(row)] + [xor_send(part(row ^ k), "row", k) for k in (1, 2, 3)]
    return pick(got, row ^ source)


def spread(panel, source):
    return lax.psum(jnp.where(lax.axis_index("col") == source, panel, 0.0), "col")


def blocks_of(rows, cols):
    return [(i, j) for i in range(rows // BLK) for j in range(cols // BLK)]


def pack_kernel(slots, value, packed):
    for b, (i, j) in enumerate(blocks_of(*value.shape)):
        slot = slots[b]

        @pl.when(slot >= 0)
        def _():
            packed[slot] = value[i * BLK : (i + 1) * BLK, j * BLK : (j + 1) * BLK]


def add_kernel(slots, value, packed, out):
    for b, (i, j) in enumerate(blocks_of(*value.shape)):
        slot = slots[b]
        at = (slice(i * BLK, (i + 1) * BLK), slice(j * BLK, (j + 1) * BLK))

        @pl.when(slot >= 0)
        def _():
            out[at] = value[at] + packed[slot]

        @pl.when(slot < 0)
        def _():
            out[at] = value[at]


SMEM = pl.BlockSpec(memory_space=pltpu.SMEM)
VMEM = pl.BlockSpec(memory_space=pltpu.VMEM)
PARAMS = pltpu.CompilerParams(vmem_limit_bytes=24 * 2**20)


def pack(slots, value, size):
    return pl.pallas_call(
        pack_kernel,
        out_shape=jax.ShapeDtypeStruct((size, BLK, BLK), jnp.float32),
        in_specs=[SMEM, VMEM],
        out_specs=VMEM,
        compiler_params=PARAMS,
    )(slots, value)


def add_packed(slots, value, packed):
    return pl.pallas_call(
        add_kernel,
        out_shape=jax.ShapeDtypeStruct(value.shape, jnp.float32),
        in_specs=[SMEM, VMEM, VMEM],
        out_specs=VMEM,
        compiler_params=PARAMS,
    )(slots, value, packed)


def slots_of(wanted):
    flat = wanted.reshape(-1).astype(jnp.int32)
    return jnp.where(flat > 0, jnp.cumsum(flat) - 1, -1), jnp.sum(flat)


def listed_exchange(acc, wanted_here, wanted_there, mask):
    to_send, n_send = slots_of(wanted_there)
    to_add, n_add = slots_of(wanted_here)
    most = to_send.shape[0]

    def branch(size, value):
        packed = pack(to_send, value, size)
        return add_packed(to_add, value, xor_send(packed, "layer", mask))

    choices = [lambda value: value]
    choices += [functools.partial(branch, s) for s in range(STEP, most + 1, STEP)]
    return lax.switch((jnp.maximum(n_send, n_add) + STEP - 1) // STEP, choices, acc)


def body(front, inverses, pattern, order, lists):
    matrix = front[0]
    rows, cols = matrix.shape
    row = lax.axis_index("row")
    col = lax.axis_index("col")
    layer = lax.axis_index("layer")
    q0, q1 = order[0], order[1]
    rb, cb = rows // BLK, cols // BLK
    row_first, col_first = row * rb, col * cb
    half = rows // 2
    quarter = cols // 4

    panels = jnp.arange(F // P_SIZE)
    alive0 = (panels != q0).astype(jnp.float32)
    alive1 = alive0 * (panels != q1).astype(jnp.float32)
    a0 = jnp.repeat(alive0, PB)
    a1 = jnp.repeat(alive1, PB)
    here = ((row_first, col_first), (rb, cb))
    mask0 = lax.dynamic_slice(pattern[0].astype(jnp.float32) * a0[:, None] * a0[None, :], *here)
    mask1 = lax.dynamic_slice(pattern[1].astype(jnp.float32) * a1[:, None] * a1[None, :], *here)
    kept = lax.dynamic_slice(a1[:, None] * a1[None, :], *here)

    left = spread(matrix, q0)
    mine = lax.dynamic_slice(lists[0], *here)
    theirs = xor_send(mine, "layer", 2)
    listed = [mine] + [xor_send(mine, "layer", 4 * k) for k in (1, 2, 3)]
    inv = jnp.concatenate(gather_row(inverses[0], row), axis=1)
    candidate = lax.dynamic_slice_in_dim(matrix, (q0 % 2) * half, half, 0)
    scaled = matmul(inv[0], exchange_row(candidate, row, q0 // 2))
    right = jnp.concatenate(gather_row(scaled, row), axis=1)
    right, theirs, listed = lax.optimization_barrier((right, theirs, listed))
    matrix = matrix - by_blocks(matmul(left, right), mask0)

    left = spread(matrix, q1)
    candidate = lax.dynamic_slice_in_dim(matrix, (q1 % 2) * half, half, 0)
    scaled = matmul(inv[1], exchange_row(candidate, row, q1 // 2))
    right = jnp.concatenate(gather_row(scaled, row), axis=1)
    acc = by_blocks(matrix - by_blocks(matmul(left, right), mask1), kept)

    def bit(values, b):
        return (values // 2**b % 2).astype(jnp.float32)

    acc = acc + by_blocks(xor_send(acc, "layer", 1), bit(mine, 0))

    acc = listed_exchange(acc, bit(mine, 1) * kept > 0, bit(theirs, 1) * kept > 0, 2)

    yy = layer // 4
    qrows = rows // 4
    qb = rb // 4
    quarters = acc.reshape(4, qrows, cols)

    def own(q):
        return lax.dynamic_index_in_dim(quarters, q, 0, keepdims=False)

    held = [own(yy)] + [xor_send(own(yy ^ k), "layer", 4 * k) for k in (1, 2, 3)]
    w = [lax.dynamic_slice_in_dim(values, yy * qb, qb, 0) for values in listed]
    for b in (2, 3):
        d = b - 1
        held = [held[k] + by_blocks(held[k ^ d], bit(w[k], b)) for k in range(4)]
    back = [held[0]] + [xor_send(held[k], "layer", 4 * k) for k in (1, 2, 3)]
    out = jnp.zeros((4, qrows, cols), jnp.float32)
    for k in range(4):
        out = lax.dynamic_update_index_in_dim(out, back[k], yy ^ k, 0)
    return out.reshape(1, rows, cols)


def solution(mesh):
    placed = (
        P("layer", "row", "col"),
        P("layer", None, "row", None),
        P(),
        P(),
        P("layer", None, None),
    )
    return jax.shard_map(
        body, mesh=mesh, in_specs=placed, out_specs=P("layer", "row", "col"), check_vma=False
    )
```

```python
import functools

import jax
import jax.numpy as jnp
from jax import lax
from jax.experimental import pallas as pl
from jax.experimental.pallas import tpu as pltpu
from jax.sharding import PartitionSpec as P

F = 4096
P_SIZE = 512
BLK = 128
PB = P_SIZE // BLK
STEP = 2
Y_GROUPS = [[first + 4 * k for k in range(4)] for first in range(4)]


def matmul(left_side, right_side):
    return jnp.dot(
        left_side,
        right_side,
        precision=lax.Precision.HIGH,
        preferred_element_type=jnp.float32,
    )


def xor_send(value, axis, mask):
    pairs = [(source, source ^ mask) for source in range(lax.axis_size(axis))]
    return lax.ppermute(value, axis, pairs)


def pick(parts, index):
    out = parts[0]
    for k in range(1, len(parts)):
        out = jnp.where(index == k, parts[k], out)
    return out


def by_blocks(value, weights):
    rows, cols = value.shape
    wide = jnp.repeat(weights, BLK, axis=1)
    return (value.reshape(rows // BLK, BLK, cols) * wide[:, None, :]).reshape(rows, cols)


def gather_row(part, row):
    got = [part] + [xor_send(part, "row", k) for k in (1, 2, 3)]
    return [pick(got, row ^ q) for q in range(4)]


def exchange_row(candidate, row, source):
    quarter = candidate.shape[1] // 4

    def part(q):
        return lax.dynamic_slice_in_dim(candidate, q * quarter, quarter, 1)

    got = [part(row)] + [xor_send(part(row ^ k), "row", k) for k in (1, 2, 3)]
    return pick(got, row ^ source)


def own_panel(panel, source):
    return jnp.where(lax.axis_index("col") == source, panel, 0.0)


def blocks_of(rows, cols):
    return [(i, j) for i in range(rows // BLK) for j in range(cols // BLK)]


def pack_kernel(slots, value, packed):
    for b, (i, j) in enumerate(blocks_of(*value.shape)):
        slot = slots[b]

        @pl.when(slot >= 0)
        def _():
            packed[slot] = value[i * BLK : (i + 1) * BLK, j * BLK : (j + 1) * BLK]


def add_kernel(slots, value, packed, out):
    for b, (i, j) in enumerate(blocks_of(*value.shape)):
        slot = slots[b]
        at = (slice(i * BLK, (i + 1) * BLK), slice(j * BLK, (j + 1) * BLK))

        @pl.when(slot >= 0)
        def _():
            out[at] = value[at] + packed[slot]

        @pl.when(slot < 0)
        def _():
            out[at] = value[at]


SMEM = pl.BlockSpec(memory_space=pltpu.SMEM)
VMEM = pl.BlockSpec(memory_space=pltpu.VMEM)
PARAMS = pltpu.CompilerParams(vmem_limit_bytes=24 * 2**20)


def pack(slots, value, size):
    return pl.pallas_call(
        pack_kernel,
        out_shape=jax.ShapeDtypeStruct((size, BLK, BLK), jnp.float32),
        in_specs=[SMEM, VMEM],
        out_specs=VMEM,
        compiler_params=PARAMS,
    )(slots, value)


def add_packed(slots, value, packed):
    return pl.pallas_call(
        add_kernel,
        out_shape=jax.ShapeDtypeStruct(value.shape, jnp.float32),
        in_specs=[SMEM, VMEM, VMEM],
        out_specs=VMEM,
        compiler_params=PARAMS,
    )(slots, value, packed)


def slots_of(wanted):
    flat = wanted.reshape(-1).astype(jnp.int32)
    return jnp.where(flat > 0, jnp.cumsum(flat) - 1, -1), jnp.sum(flat)


def listed_exchange(acc, wanted_here, wanted_there, mask):
    to_send, n_send = slots_of(wanted_there)
    to_add, n_add = slots_of(wanted_here)
    most = to_send.shape[0]

    def branch(size, value):
        packed = pack(to_send, value, size)
        return add_packed(to_add, value, xor_send(packed, "layer", mask))

    choices = [lambda value: value]
    choices += [functools.partial(branch, s) for s in range(STEP, most + 1, STEP)]
    return lax.switch((jnp.maximum(n_send, n_add) + STEP - 1) // STEP, choices, acc)


def body(front, inverses, pattern, order, lists):
    matrix = front[0]
    rows, cols = matrix.shape
    row = lax.axis_index("row")
    col = lax.axis_index("col")
    layer = lax.axis_index("layer")
    q0, q1 = order[0], order[1]
    rb, cb = rows // BLK, cols // BLK
    row_first, col_first = row * rb, col * cb
    half = rows // 2
    quarter = cols // 4

    panels = jnp.arange(F // P_SIZE)
    alive0 = (panels != q0).astype(jnp.float32)
    alive1 = alive0 * (panels != q1).astype(jnp.float32)
    a0 = jnp.repeat(alive0, PB)
    a1 = jnp.repeat(alive1, PB)
    here = ((row_first, col_first), (rb, cb))
    mask0 = lax.dynamic_slice(pattern[0].astype(jnp.float32) * a0[:, None] * a0[None, :], *here)
    mask1 = lax.dynamic_slice(pattern[1].astype(jnp.float32) * a1[:, None] * a1[None, :], *here)
    kept = lax.dynamic_slice(a1[:, None] * a1[None, :], *here)

    panel, matrix = lax.optimization_barrier((own_panel(matrix, q0), matrix))
    left = lax.psum(panel, "col")
    candidate = lax.dynamic_slice_in_dim(matrix, (q0 % 2) * half, half, 0)
    pivot, inverse_part = lax.optimization_barrier(
        (exchange_row(candidate, row, q0 // 2), inverses[0])
    )
    inv = jnp.concatenate(gather_row(inverse_part, row), axis=1)
    scaled = matmul(inv[0], pivot)
    right = jnp.concatenate(gather_row(scaled, row), axis=1)
    matrix = matrix - by_blocks(matmul(left, right), mask0)

    panel, matrix = lax.optimization_barrier((own_panel(matrix, q1), matrix))
    left = lax.psum(panel, "col")
    candidate = lax.dynamic_slice_in_dim(matrix, (q1 % 2) * half, half, 0)
    pivot, listed = lax.optimization_barrier((exchange_row(candidate, row, q1 // 2), lists[0]))
    scaled = matmul(inv[1], pivot)
    right = jnp.concatenate(gather_row(scaled, row), axis=1)
    mine = lax.dynamic_slice(listed, *here)
    theirs = xor_send(mine, "layer", 2)
    listed = lax.all_gather(mine, "layer", axis_index_groups=Y_GROUPS)
    left, right, theirs, listed = lax.optimization_barrier((left, right, theirs, listed))
    acc = by_blocks(matrix - by_blocks(matmul(left, right), mask1), kept)

    def bit(values, b):
        return (values // 2**b % 2).astype(jnp.float32)

    acc = acc + by_blocks(xor_send(acc, "layer", 1), bit(mine, 0))

    acc = listed_exchange(acc, bit(mine, 1) * kept > 0, bit(theirs, 1) * kept > 0, 2)

    yy = layer // 4
    qb = rb // 4

    def turn(value):
        return lax.all_to_all(
            value.reshape(4, -1, cols), "layer", 0, 0, axis_index_groups=Y_GROUPS, tiled=True
        )

    held = turn(acc)
    held = [held[k] for k in range(4)]
    w = lax.dynamic_slice_in_dim(listed, yy * qb, qb, 1)
    for b in (2, 3):
        d = b - 1
        held = [held[k] + by_blocks(held[k ^ d], bit(w[k], b)) for k in range(4)]
    return turn(jnp.stack(held)).reshape(1, rows, cols)


def solution(mesh):
    placed = (
        P("layer", "row", "col"),
        P("layer", None, "row", None),
        P(),
        P(),
        P("layer", None, None),
    )
    return jax.shard_map(
        body, mesh=mesh, in_specs=placed, out_specs=P("layer", "row", "col"), check_vma=False
    )
```

```python
import functools

import jax
import jax.numpy as jnp
from jax import lax
from jax.experimental import pallas as pl
from jax.experimental.pallas import tpu as pltpu
from jax.sharding import PartitionSpec as P

F = 4096
P_SIZE = 512
BLK = 128
PB = P_SIZE // BLK
STEP = 2
Y_GROUPS = [[first + 4 * k for k in range(4)] for first in range(4)]


def matmul(left_side, right_side):
    return jnp.dot(
        left_side,
        right_side,
        precision=lax.Precision.HIGH,
        preferred_element_type=jnp.float32,
    )


def xor_send(value, axis, mask):
    pairs = [(source, source ^ mask) for source in range(lax.axis_size(axis))]
    return lax.ppermute(value, axis, pairs)


def pick(parts, index):
    out = parts[0]
    for k in range(1, len(parts)):
        out = jnp.where(index == k, parts[k], out)
    return out


def by_blocks(value, weights):
    rows, cols = value.shape
    wide = jnp.repeat(weights, BLK, axis=1)
    return (value.reshape(rows // BLK, BLK, cols) * wide[:, None, :]).reshape(rows, cols)


def gather_row(part, row):
    got = [part] + [xor_send(part, "row", k) for k in (1, 2, 3)]
    return [pick(got, row ^ q) for q in range(4)]


def exchange_row(candidates, row, sources):
    part_rows = candidates.shape[1] // 4

    def part(r):
        return lax.dynamic_slice_in_dim(candidates, r * part_rows, part_rows, 1)

    got = [part(row)] + [xor_send(part(row ^ k), "row", k) for k in (1, 2, 3)]
    return [pick([g[i] for g in got], row ^ source) for i, source in enumerate(sources)]


def spread_part(value, col, source):
    for bit in (4, 2, 1):
        got = lax.cond(
            ((col ^ source) & (bit - 1)) == 0,
            lambda held, bit=bit: xor_send(held, "col", bit),
            lambda held: held,
            value,
        )
        value = jnp.where(((col ^ source) & bit) != 0, got, value)
    return value


def blocks_of(rows, cols):
    return [(i, j) for i in range(rows // BLK) for j in range(cols // BLK)]


def pack_kernel(slots, value, packed):
    for b, (i, j) in enumerate(blocks_of(*value.shape)):
        slot = slots[b]

        @pl.when(slot >= 0)
        def _():
            packed[slot] = value[i * BLK : (i + 1) * BLK, j * BLK : (j + 1) * BLK]


def add_kernel(slots, value, packed, out):
    for b, (i, j) in enumerate(blocks_of(*value.shape)):
        slot = slots[b]
        at = (slice(i * BLK, (i + 1) * BLK), slice(j * BLK, (j + 1) * BLK))

        @pl.when(slot >= 0)
        def _():
            out[at] = value[at] + packed[slot]

        @pl.when(slot < 0)
        def _():
            out[at] = value[at]


SMEM = pl.BlockSpec(memory_space=pltpu.SMEM)
VMEM = pl.BlockSpec(memory_space=pltpu.VMEM)
PARAMS = pltpu.CompilerParams(vmem_limit_bytes=24 * 2**20)


def pack(slots, value, size):
    return pl.pallas_call(
        pack_kernel,
        out_shape=jax.ShapeDtypeStruct((size, BLK, BLK), jnp.float32),
        in_specs=[SMEM, VMEM],
        out_specs=VMEM,
        compiler_params=PARAMS,
    )(slots, value)


def add_packed(slots, value, packed):
    return pl.pallas_call(
        add_kernel,
        out_shape=jax.ShapeDtypeStruct(value.shape, jnp.float32),
        in_specs=[SMEM, VMEM, VMEM],
        out_specs=VMEM,
        compiler_params=PARAMS,
    )(slots, value, packed)


def slots_of(wanted):
    flat = wanted.reshape(-1).astype(jnp.int32)
    return jnp.where(flat > 0, jnp.cumsum(flat) - 1, -1), jnp.sum(flat)


def listed_exchange(acc, wanted_here, wanted_there, mask):
    to_send, n_send = slots_of(wanted_there)
    to_add, n_add = slots_of(wanted_here)
    most = to_send.shape[0]

    def branch(size, value):
        packed = pack(to_send, value, size)
        return add_packed(to_add, value, xor_send(packed, "layer", mask))

    choices = [lambda value: value]
    choices += [functools.partial(branch, s) for s in range(STEP, most + 1, STEP)]
    return lax.switch((jnp.maximum(n_send, n_add) + STEP - 1) // STEP, choices, acc)


def body(front, inverses, pattern, order, lists):
    matrix = front[0]
    rows, cols = matrix.shape
    row = lax.axis_index("row")
    col = lax.axis_index("col")
    layer = lax.axis_index("layer")
    q0, q1 = order[0], order[1]
    rb, cb = rows // BLK, cols // BLK
    row_first, col_first = row * rb, col * cb
    half = rows // 2

    panels = jnp.arange(F // P_SIZE)
    alive0 = (panels != q0).astype(jnp.float32)
    alive1 = alive0 * (panels != q1).astype(jnp.float32)
    a0 = jnp.repeat(alive0, PB)
    a1 = jnp.repeat(alive1, PB)
    here = ((row_first, col_first), (rb, cb))
    mask0 = lax.dynamic_slice(pattern[0].astype(jnp.float32) * a0[:, None] * a0[None, :], *here)
    mask1 = lax.dynamic_slice(pattern[1].astype(jnp.float32) * a1[:, None] * a1[None, :], *here)
    kept = lax.dynamic_slice(a1[:, None] * a1[None, :], *here)

    mask_c = lax.dynamic_slice(
        pattern[0].astype(jnp.float32) * a0[:, None] * a0[None, :],
        (row_first, q1 * PB),
        (rb, PB),
    )
    mask_r = lax.dynamic_slice(
        pattern[0].astype(jnp.float32) * a0[:, None] * a0[None, :],
        (q1 * PB, col_first),
        (PB, cb),
    )

    panel0 = jnp.where(col == q0, matrix, 0.0)
    panel1 = jnp.where(col == q1, matrix, 0.0)
    panel0, panel1, matrix = lax.optimization_barrier((panel0, panel1, matrix))
    left0, column1 = lax.psum((panel0, panel1), "col")

    candidates = jnp.stack(
        [
            lax.dynamic_slice_in_dim(matrix, (q0 % 2) * half, half, 0),
            lax.dynamic_slice_in_dim(matrix, (q1 % 2) * half, half, 0),
        ]
    )
    part0, part1, inverse_part, listed = lax.optimization_barrier(
        (*exchange_row(candidates, row, (q0 // 2, q1 // 2)), inverses[0], lists[0])
    )
    rows01 = jnp.concatenate(gather_row(jnp.stack([part0, part1]), row), axis=1)
    inv = jnp.concatenate(gather_row(inverse_part, row), axis=1)
    x_part = spread_part(part0, col, q1)
    y_part = spread_part(part1, col, q0)
    crossed = jnp.concatenate(gather_row(jnp.stack([x_part, y_part]), row), axis=1)
    mine = lax.dynamic_slice(listed, *here)
    theirs = xor_send(mine, "layer", 2)
    listed = lax.all_gather(mine, "layer", axis_index_groups=Y_GROUPS)

    right0 = matmul(inv[0], rows01[0])
    right0x = matmul(inv[0], crossed[0])
    right1 = matmul(inv[1], rows01[1] - by_blocks(matmul(crossed[1], right0), mask_r))
    right0, right0x, right1, theirs, listed, left0, column1 = lax.optimization_barrier(
        (right0, right0x, right1, theirs, listed, left0, column1)
    )

    left1 = column1 - by_blocks(matmul(left0, right0x), mask_c)
    matrix = matrix - by_blocks(matmul(left0, right0), mask0)
    acc = by_blocks(matrix - by_blocks(matmul(left1, right1), mask1), kept)

    def bit(values, b):
        return (values // 2**b % 2).astype(jnp.float32)

    acc = acc + by_blocks(xor_send(acc, "layer", 1), bit(mine, 0))

    acc = listed_exchange(acc, bit(mine, 1) * kept > 0, bit(theirs, 1) * kept > 0, 2)

    yy = layer // 4
    qb = rb // 4

    def turn(value):
        return lax.all_to_all(
            value.reshape(4, -1, cols), "layer", 0, 0, axis_index_groups=Y_GROUPS, tiled=True
        )

    held = turn(acc)
    held = [held[k] for k in range(4)]
    w = lax.dynamic_slice_in_dim(listed, yy * qb, qb, 1)
    for b in (2, 3):
        d = b - 1
        held = [held[k] + by_blocks(held[k ^ d], bit(w[k], b)) for k in range(4)]
    return turn(jnp.stack(held)).reshape(1, rows, cols)


def solution(mesh):
    placed = (
        P("layer", "row", "col"),
        P("layer", None, "row", None),
        P(),
        P(),
        P("layer", None, None),
    )
    return jax.shard_map(
        body, mesh=mesh, in_specs=placed, out_specs=P("layer", "row", "col"), check_vma=False
    )
```

```python
import functools

import jax
import jax.numpy as jnp
from jax import lax
from jax.experimental import pallas as pl
from jax.experimental.pallas import tpu as pltpu
from jax.sharding import PartitionSpec as P

F = 4096
P_SIZE = 512
BLK = 128
PB = P_SIZE // BLK
SIZES = (3, 6, 8, *range(9, 25), 26, 28, 30, 32)
Y_GROUPS = [[first + 4 * k for k in range(4)] for first in range(4)]


def matmul(left_side, right_side):
    return jnp.dot(
        left_side,
        right_side,
        precision=lax.Precision.HIGH,
        preferred_element_type=jnp.float32,
    )


def xor_send(value, axis, mask):
    pairs = [(source, source ^ mask) for source in range(lax.axis_size(axis))]
    return lax.ppermute(value, axis, pairs)


def pick(parts, index):
    out = parts[0]
    for k in range(1, len(parts)):
        out = jnp.where(index == k, parts[k], out)
    return out


def by_blocks(value, weights):
    rows, cols = value.shape
    wide = jnp.repeat(weights, BLK, axis=1)
    return (value.reshape(rows // BLK, BLK, cols) * wide[:, None, :]).reshape(rows, cols)


def gather_row(part, row):
    got = [part] + [xor_send(part, "row", k) for k in (1, 2, 3)]
    return [pick(got, row ^ q) for q in range(4)]


def exchange_row(candidates, row, sources):
    part_rows = candidates.shape[1] // 4

    def part(r):
        return lax.dynamic_slice_in_dim(candidates, r * part_rows, part_rows, 1)

    got = [part(row)] + [xor_send(part(row ^ k), "row", k) for k in (1, 2, 3)]
    return [pick([g[i] for g in got], row ^ source) for i, source in enumerate(sources)]


def spread_part(value, col, source):
    for bit in (4, 2, 1):
        got = lax.cond(
            ((col ^ source) & (bit - 1)) == 0,
            lambda held, bit=bit: xor_send(held, "col", bit),
            lambda held: held,
            value,
        )
        value = jnp.where(((col ^ source) & bit) != 0, got, value)
    return value


def over_blocks(shape, step):
    per_row = shape[1] // BLK

    def one(b, _):
        row_start = pl.multiple_of(b // per_row * BLK, BLK)
        col_start = pl.multiple_of(b % per_row * BLK, BLK)
        step(b, (pl.ds(row_start, BLK), pl.ds(col_start, BLK)))
        return 0

    lax.fori_loop(0, shape[0] // BLK * per_row, one, 0)


def pack_kernel(taken, slots, value, other, packed, merged):
    def step(b, at):
        merged[at] = value[at]

        @pl.when(taken[b] > 0)
        def _():
            merged[at] = merged[at] + other[at]

        slot = slots[b]

        @pl.when(slot >= 0)
        def _():
            packed[slot] = merged[at]

    over_blocks(value.shape, step)


def add_kernel(slots, value, packed, out):
    def step(b, at):
        out[at] = value[at]
        slot = slots[b]

        @pl.when(slot >= 0)
        def _():
            out[at] = out[at] + packed[slot]

    over_blocks(value.shape, step)


SMEM = pl.BlockSpec(memory_space=pltpu.SMEM)
VMEM = pl.BlockSpec(memory_space=pltpu.VMEM)
PARAMS = pltpu.CompilerParams(vmem_limit_bytes=24 * 2**20)


def pack(taken, slots, value, other, size):
    return pl.pallas_call(
        pack_kernel,
        out_shape=(
            jax.ShapeDtypeStruct((size, BLK, BLK), jnp.float32),
            jax.ShapeDtypeStruct(value.shape, jnp.float32),
        ),
        in_specs=[SMEM, SMEM, VMEM, VMEM],
        out_specs=(VMEM, VMEM),
        compiler_params=PARAMS,
    )(taken, slots, value, other)


def add_packed(slots, value, packed):
    return pl.pallas_call(
        add_kernel,
        out_shape=jax.ShapeDtypeStruct(value.shape, jnp.float32),
        in_specs=[SMEM, VMEM, VMEM],
        out_specs=VMEM,
        compiler_params=PARAMS,
    )(slots, value, packed)


def slots_of(wanted):
    flat = wanted.reshape(-1).astype(jnp.int32)
    return jnp.where(flat > 0, jnp.cumsum(flat) - 1, -1), jnp.sum(flat)


def listed_exchange(value, other, taken, wanted_here, wanted_there, mask):
    to_send, n_send = slots_of(wanted_there)
    to_add, n_add = slots_of(wanted_here)
    taken_flat = taken.reshape(-1).astype(jnp.int32)

    def alone(value, other):
        return value + by_blocks(other, taken)

    def branch(size, value, other):
        packed, merged = pack(taken_flat, to_send, value, other, size)
        return add_packed(to_add, merged, xor_send(packed, "layer", mask))

    choices = [alone] + [functools.partial(branch, size) for size in SIZES]
    needed = jnp.maximum(n_send, n_add)
    index = (needed > jnp.array((0, *SIZES), jnp.int32)).sum().astype(jnp.int32)
    return lax.switch(index, choices, value, other)


def body(front, inverses, pattern, order, lists):
    matrix = front[0]
    rows, cols = matrix.shape
    row = lax.axis_index("row")
    col = lax.axis_index("col")
    layer = lax.axis_index("layer")
    q0, q1 = order[0], order[1]
    rb, cb = rows // BLK, cols // BLK
    row_first, col_first = row * rb, col * cb
    half = rows // 2

    panels = jnp.arange(F // P_SIZE)
    alive0 = (panels != q0).astype(jnp.float32)
    alive1 = alive0 * (panels != q1).astype(jnp.float32)
    a0 = jnp.repeat(alive0, PB)
    a1 = jnp.repeat(alive1, PB)
    here = ((row_first, col_first), (rb, cb))
    mask0 = lax.dynamic_slice(pattern[0].astype(jnp.float32) * a0[:, None] * a0[None, :], *here)
    mask1 = lax.dynamic_slice(pattern[1].astype(jnp.float32) * a1[:, None] * a1[None, :], *here)
    kept = lax.dynamic_slice(a1[:, None] * a1[None, :], *here)

    mask_c = lax.dynamic_slice(
        pattern[0].astype(jnp.float32) * a0[:, None] * a0[None, :],
        (row_first, q1 * PB),
        (rb, PB),
    )
    mask_r = lax.dynamic_slice(
        pattern[0].astype(jnp.float32) * a0[:, None] * a0[None, :],
        (q1 * PB, col_first),
        (PB, cb),
    )

    panel0 = jnp.where(col == q0, matrix, 0.0)
    panel1 = jnp.where(col == q1, matrix, 0.0)
    panel0, panel1, matrix, listed = lax.optimization_barrier((panel0, panel1, matrix, lists[0]))
    left0, column1 = lax.psum((panel0, panel1), "col")
    mine = lax.dynamic_slice(listed, *here)
    theirs = xor_send(mine, "layer", 2)
    theirs, matrix = lax.optimization_barrier((theirs, matrix))

    candidates = jnp.stack(
        [
            lax.dynamic_slice_in_dim(matrix, (q0 & 1) * half, half, 0),
            lax.dynamic_slice_in_dim(matrix, (q1 & 1) * half, half, 0),
        ]
    )
    part0, part1, inverse_part = lax.optimization_barrier(
        (*exchange_row(candidates, row, (q0 >> 1, q1 >> 1)), inverses[0])
    )
    rows01 = jnp.concatenate(gather_row(jnp.stack([part0, part1]), row), axis=1)
    inv = jnp.concatenate(gather_row(inverse_part, row), axis=1)
    x_part = spread_part(part0, col, q1)
    y_part = spread_part(part1, col, q0)
    crossed = jnp.concatenate(gather_row(jnp.stack([x_part, y_part]), row), axis=1)
    listed = lax.all_gather(mine, "layer", axis_index_groups=Y_GROUPS)

    right0 = matmul(inv[0], rows01[0])
    right0x = matmul(inv[0], crossed[0])
    right1 = matmul(inv[1], rows01[1] - by_blocks(matmul(crossed[1], right0), mask_r))
    right0, right0x, right1, theirs, listed, left0, column1 = lax.optimization_barrier(
        (right0, right0x, right1, theirs, listed, left0, column1)
    )

    left1 = column1 - by_blocks(matmul(left0, right0x), mask_c)
    matrix = matrix - by_blocks(matmul(left0, right0), mask0)
    acc = by_blocks(matrix - by_blocks(matmul(left1, right1), mask1), kept)

    def bit(values, b):
        return (values // 2**b % 2).astype(jnp.float32)

    acc = listed_exchange(
        acc,
        xor_send(acc, "layer", 1),
        bit(mine, 0),
        bit(mine, 1) * kept > 0,
        bit(theirs, 1) * kept > 0,
        2,
    )

    yy = layer // 4
    qb = rb // 4

    def turn(value):
        return lax.all_to_all(
            value.reshape(4, -1, cols), "layer", 0, 0, axis_index_groups=Y_GROUPS, tiled=True
        )

    held = turn(acc)
    held = [held[k] for k in range(4)]
    w = lax.dynamic_slice_in_dim(listed, yy * qb, qb, 1)
    for b in (2, 3):
        d = b - 1
        held = [held[k] + by_blocks(held[k ^ d], bit(w[k], b)) for k in range(4)]
    return turn(jnp.stack(held)).reshape(1, rows, cols)


def solution(mesh):
    placed = (
        P("layer", "row", "col"),
        P("layer", None, "row", None),
        P(),
        P(),
        P("layer", None, None),
    )
    return jax.shard_map(
        body, mesh=mesh, in_specs=placed, out_specs=P("layer", "row", "col"), check_vma=False
    )
```

```python
import functools

import jax
import jax.numpy as jnp
from jax import lax
from jax.experimental import pallas as pl
from jax.experimental.pallas import tpu as pltpu
from jax.sharding import PartitionSpec as P

F = 4096
P_SIZE = 512
BLK = 128
PB = P_SIZE // BLK
SIZES = (3, 6, 8, *range(9, 25), 26, 28, 30, 32)
Y_GROUPS = [[first + 4 * k for k in range(4)] for first in range(4)]


def matmul(left_side, right_side):
    return jnp.dot(
        left_side,
        right_side,
        precision=lax.Precision.HIGH,
        preferred_element_type=jnp.float32,
    )


def xor_send(value, axis, mask):
    pairs = [(source, source ^ mask) for source in range(lax.axis_size(axis))]
    return lax.ppermute(value, axis, pairs)


def pick(parts, index):
    out = parts[0]
    for k in range(1, len(parts)):
        out = jnp.where(index == k, parts[k], out)
    return out


def by_blocks(value, weights):
    rows, cols = value.shape
    wide = jnp.repeat(weights, BLK, axis=1)
    return (value.reshape(rows // BLK, BLK, cols) * wide[:, None, :]).reshape(rows, cols)


def gather_row(part, row):
    got = [part] + [xor_send(part, "row", k) for k in (1, 2, 3)]
    return [pick(got, row ^ q) for q in range(4)]


def exchange_row(candidates, row, sources):
    part_rows = candidates.shape[1] // 4

    def part(r):
        return lax.dynamic_slice_in_dim(candidates, r * part_rows, part_rows, 1)

    got = [part(row)] + [xor_send(part(row ^ k), "row", k) for k in (1, 2, 3)]
    return [pick([g[i] for g in got], row ^ source) for i, source in enumerate(sources)]


def spread_part(value, col, source):
    for bit in (4, 2, 1):
        got = lax.cond(
            ((col ^ source) & (bit - 1)) == 0,
            lambda held, bit=bit: xor_send(held, "col", bit),
            lambda held: held,
            value,
        )
        value = jnp.where(((col ^ source) & bit) != 0, got, value)
    return value


def over_blocks(shape, step):
    per_row = shape[1] // BLK

    def one(b, _):
        row_start = pl.multiple_of(b // per_row * BLK, BLK)
        col_start = pl.multiple_of(b % per_row * BLK, BLK)
        step(b, (pl.ds(row_start, BLK), pl.ds(col_start, BLK)))
        return 0

    lax.fori_loop(0, shape[0] // BLK * per_row, one, 0)


def pack_kernel(taken, slots, value, other, packed, merged):
    def step(b, at):
        block = value[at] + other[at] * taken[b].astype(jnp.float32)
        merged[at] = block
        slot = slots[b]

        @pl.when(slot >= 0)
        def _():
            packed[slot] = block

    over_blocks(value.shape, step)


def add_kernel(slots, value, packed, out):
    def step(b, at):
        slot = slots[b]

        @pl.when(slot >= 0)
        def _():
            out[at] = value[at] + packed[slot]

        @pl.when(slot < 0)
        def _():
            out[at] = value[at]

    over_blocks(value.shape, step)


SMEM = pl.BlockSpec(memory_space=pltpu.SMEM)
VMEM = pl.BlockSpec(memory_space=pltpu.VMEM)
PARAMS = pltpu.CompilerParams(vmem_limit_bytes=24 * 2**20)


def pack(taken, slots, value, other, size):
    return pl.pallas_call(
        pack_kernel,
        out_shape=(
            jax.ShapeDtypeStruct((size, BLK, BLK), jnp.float32),
            jax.ShapeDtypeStruct(value.shape, jnp.float32),
        ),
        in_specs=[SMEM, SMEM, VMEM, VMEM],
        out_specs=(VMEM, VMEM),
        compiler_params=PARAMS,
    )(taken, slots, value, other)


def add_packed(slots, value, packed):
    return pl.pallas_call(
        add_kernel,
        out_shape=jax.ShapeDtypeStruct(value.shape, jnp.float32),
        in_specs=[SMEM, VMEM, VMEM],
        out_specs=VMEM,
        compiler_params=PARAMS,
    )(slots, value, packed)


def slots_of(wanted):
    flat = wanted.reshape(-1).astype(jnp.int32)
    return jnp.where(flat > 0, jnp.cumsum(flat) - 1, -1), jnp.sum(flat)


def plan_exchange(wanted_here, wanted_there):
    to_send, n_send = slots_of(wanted_there)
    to_add, n_add = slots_of(wanted_here)
    needed = jnp.maximum(n_send, n_add)
    index = (needed > jnp.array((0, *SIZES), jnp.int32)).sum().astype(jnp.int32)
    return to_send, to_add, index


def listed_exchange(value, other, taken, plan, mask):
    to_send, to_add, index = plan

    def alone(value, other):
        return value + by_blocks(other, taken.reshape(-1, value.shape[1] // BLK).astype(jnp.float32))

    def branch(size, value, other):
        packed, merged = pack(taken, to_send, value, other, size)
        return add_packed(to_add, merged, xor_send(packed, "layer", mask))

    choices = [alone] + [functools.partial(branch, size) for size in SIZES]
    return lax.switch(index, choices, value, other)


def body(front, inverses, pattern, order, lists):
    matrix = front[0]
    rows, cols = matrix.shape
    row = lax.axis_index("row")
    col = lax.axis_index("col")
    layer = lax.axis_index("layer")
    q0, q1 = order[0], order[1]
    rb, cb = rows // BLK, cols // BLK
    row_first, col_first = row * rb, col * cb
    half = rows // 2

    panels = jnp.arange(F // P_SIZE)
    alive0 = (panels != q0).astype(jnp.float32)
    alive1 = alive0 * (panels != q1).astype(jnp.float32)
    a0 = jnp.repeat(alive0, PB)
    a1 = jnp.repeat(alive1, PB)
    here = ((row_first, col_first), (rb, cb))
    mask0 = lax.dynamic_slice(pattern[0].astype(jnp.float32) * a0[:, None] * a0[None, :], *here)
    mask1 = lax.dynamic_slice(pattern[1].astype(jnp.float32) * a1[:, None] * a1[None, :], *here)
    kept = lax.dynamic_slice(a1[:, None] * a1[None, :], *here)

    mask_c = lax.dynamic_slice(
        pattern[0].astype(jnp.float32) * a0[:, None] * a0[None, :],
        (row_first, q1 * PB),
        (rb, PB),
    )
    mask_r = lax.dynamic_slice(
        pattern[0].astype(jnp.float32) * a0[:, None] * a0[None, :],
        (q1 * PB, col_first),
        (PB, cb),
    )

    panel0 = jnp.where(col == q0, matrix, 0.0)
    panel1 = jnp.where(col == q1, matrix, 0.0)
    panel0, panel1, matrix, listed = lax.optimization_barrier((panel0, panel1, matrix, lists[0]))
    left0, column1 = lax.psum((panel0, panel1), "col")
    mine = lax.dynamic_slice(listed, *here)
    theirs = xor_send(mine, "layer", 2)
    theirs, matrix = lax.optimization_barrier((theirs, matrix))

    candidates = jnp.stack(
        [
            lax.dynamic_slice_in_dim(matrix, (q0 & 1) * half, half, 0),
            lax.dynamic_slice_in_dim(matrix, (q1 & 1) * half, half, 0),
        ]
    )
    part0, part1, inverse_part = lax.optimization_barrier(
        (*exchange_row(candidates, row, (q0 >> 1, q1 >> 1)), inverses[0])
    )
    rows01 = jnp.concatenate(gather_row(jnp.stack([part0, part1]), row), axis=1)
    inv = jnp.concatenate(gather_row(inverse_part, row), axis=1)
    x_part = spread_part(part0, col, q1)
    y_part = spread_part(part1, col, q0)
    crossed = jnp.concatenate(gather_row(jnp.stack([x_part, y_part]), row), axis=1)
    listed = lax.all_gather(mine, "layer", axis_index_groups=Y_GROUPS)

    right0 = matmul(inv[0], rows01[0])
    right0x = matmul(inv[0], crossed[0])
    right1 = matmul(inv[1], rows01[1] - by_blocks(matmul(crossed[1], right0), mask_r))
    def bit(values, b):
        return values // 2**b % 2

    taken = bit(mine, 0).reshape(-1)
    plan = plan_exchange(bit(mine, 1) * kept > 0, bit(theirs, 1) * kept > 0)
    right0, right0x, right1, listed, taken, plan, left0, column1 = lax.optimization_barrier(
        (right0, right0x, right1, listed, taken, plan, left0, column1)
    )

    left1 = column1 - by_blocks(matmul(left0, right0x), mask_c)
    matrix = matrix - by_blocks(matmul(left0, right0), mask0)
    acc = by_blocks(matrix - by_blocks(matmul(left1, right1), mask1), kept)

    acc = listed_exchange(acc, xor_send(acc, "layer", 1), taken, plan, 2)

    yy = layer // 4
    qb = rb // 4

    def turn(value):
        return lax.all_to_all(
            value.reshape(4, -1, cols), "layer", 0, 0, axis_index_groups=Y_GROUPS, tiled=True
        )

    held = turn(acc)
    held = [held[k] for k in range(4)]
    w = lax.dynamic_slice_in_dim(listed, yy * qb, qb, 1)
    for b in (2, 3):
        d = b - 1
        held = [held[k] + by_blocks(held[k ^ d], bit(w[k], b).astype(jnp.float32)) for k in range(4)]
    return turn(jnp.stack(held)).reshape(1, rows, cols)


def solution(mesh):
    placed = (
        P("layer", "row", "col"),
        P("layer", None, "row", None),
        P(),
        P(),
        P("layer", None, None),
    )
    return jax.shard_map(
        body, mesh=mesh, in_specs=placed, out_specs=P("layer", "row", "col"), check_vma=False
    )
```

```python
import functools

import jax
import jax.numpy as jnp
from jax import lax
from jax.experimental import pallas as pl
from jax.experimental.pallas import tpu as pltpu
from jax.sharding import PartitionSpec as P

F = 4096
P_SIZE = 512
BLK = 128
PB = P_SIZE // BLK
SIZES = (3, 6, 8, *range(9, 25), 26, 28, 30, 32)
Y_GROUPS = [[first + 4 * k for k in range(4)] for first in range(4)]


def matmul(left_side, right_side):
    return jnp.dot(
        left_side,
        right_side,
        precision=lax.Precision.HIGH,
        preferred_element_type=jnp.float32,
    )


def xor_send(value, axis, mask):
    pairs = [(source, source ^ mask) for source in range(lax.axis_size(axis))]
    return lax.ppermute(value, axis, pairs)


def pick(parts, index):
    out = parts[0]
    for k in range(1, len(parts)):
        out = jnp.where(index == k, parts[k], out)
    return out


def by_blocks(value, weights):
    rows, cols = value.shape
    wide = jnp.repeat(weights, BLK, axis=1)
    return (value.reshape(rows // BLK, BLK, cols) * wide[:, None, :]).reshape(rows, cols)


def gather_row(part, row):
    got = [part] + [xor_send(part, "row", k) for k in (1, 2, 3)]
    return [pick(got, row ^ q) for q in range(4)]


def exchange_row(candidates, row, sources):
    part_rows = candidates.shape[1] // 4

    def part(r):
        return lax.dynamic_slice_in_dim(candidates, r * part_rows, part_rows, 1)

    near = xor_send(part(row ^ 1), "row", 1)
    near, candidates = lax.optimization_barrier((near, candidates))
    got = [part(row), near] + [xor_send(part(row ^ k), "row", k) for k in (2, 3)]
    return [pick([g[i] for g in got], row ^ source) for i, source in enumerate(sources)]


def spread_part(value, col, source):
    for bit in (4, 2, 1):
        got = lax.cond(
            ((col ^ source) & (bit - 1)) == 0,
            lambda held, bit=bit: xor_send(held, "col", bit),
            lambda held: held,
            value,
        )
        value = jnp.where(((col ^ source) & bit) != 0, got, value)
    return value


def over_blocks(shape, step):
    per_row = shape[1] // BLK

    def one(b, _):
        row_start = pl.multiple_of(b // per_row * BLK, BLK)
        col_start = pl.multiple_of(b % per_row * BLK, BLK)
        step(b, (pl.ds(row_start, BLK), pl.ds(col_start, BLK)))
        return 0

    lax.fori_loop(0, shape[0] // BLK * per_row, one, 0)


def pack_kernel(taken, slots, value, other, packed, merged):
    def step(b, at):
        block = value[at] + other[at] * taken[b].astype(jnp.float32)
        merged[at] = block
        slot = slots[b]

        @pl.when(slot >= 0)
        def _():
            packed[slot] = block

    over_blocks(value.shape, step)


def add_kernel(slots, value, packed, out):
    def step(b, at):
        slot = slots[b]

        @pl.when(slot >= 0)
        def _():
            out[at] = value[at] + packed[slot]

        @pl.when(slot < 0)
        def _():
            out[at] = value[at]

    over_blocks(value.shape, step)


SMEM = pl.BlockSpec(memory_space=pltpu.SMEM)
VMEM = pl.BlockSpec(memory_space=pltpu.VMEM)
PARAMS = pltpu.CompilerParams(vmem_limit_bytes=24 * 2**20)


def pack(taken, slots, value, other, size):
    return pl.pallas_call(
        pack_kernel,
        out_shape=(
            jax.ShapeDtypeStruct((size, BLK, BLK), jnp.float32),
            jax.ShapeDtypeStruct(value.shape, jnp.float32),
        ),
        in_specs=[SMEM, SMEM, VMEM, VMEM],
        out_specs=(VMEM, VMEM),
        compiler_params=PARAMS,
    )(taken, slots, value, other)


def add_packed(slots, value, packed):
    return pl.pallas_call(
        add_kernel,
        out_shape=jax.ShapeDtypeStruct(value.shape, jnp.float32),
        in_specs=[SMEM, VMEM, VMEM],
        out_specs=VMEM,
        compiler_params=PARAMS,
    )(slots, value, packed)


def slots_of(wanted):
    flat = wanted.reshape(-1).astype(jnp.int32)
    return jnp.where(flat > 0, jnp.cumsum(flat) - 1, -1), jnp.sum(flat)


def plan_exchange(wanted_here, wanted_there):
    to_send, n_send = slots_of(wanted_there)
    to_add, n_add = slots_of(wanted_here)
    needed = jnp.maximum(n_send, n_add)
    index = (needed > jnp.array((0, *SIZES), jnp.int32)).sum().astype(jnp.int32)
    return to_send, to_add, index


def listed_exchange(value, other, taken, plan, mask):
    to_send, to_add, index = plan

    def alone(value, other):
        return value + by_blocks(other, taken.reshape(-1, value.shape[1] // BLK).astype(jnp.float32))

    def branch(size, value, other):
        packed, merged = pack(taken, to_send, value, other, size)
        return add_packed(to_add, merged, xor_send(packed, "layer", mask))

    choices = [alone] + [functools.partial(branch, size) for size in SIZES]
    return lax.switch(index, choices, value, other)


def body(front, inverses, pattern, order, lists):
    matrix = front[0]
    rows, cols = matrix.shape
    row = lax.axis_index("row")
    col = lax.axis_index("col")
    layer = lax.axis_index("layer")
    q0, q1 = order[0], order[1]
    rb, cb = rows // BLK, cols // BLK
    row_first, col_first = row * rb, col * cb
    half = rows // 2

    panels = jnp.arange(F // P_SIZE)
    alive0 = (panels != q0).astype(jnp.float32)
    alive1 = alive0 * (panels != q1).astype(jnp.float32)
    a0 = jnp.repeat(alive0, PB)
    a1 = jnp.repeat(alive1, PB)
    here = ((row_first, col_first), (rb, cb))
    mask0 = lax.dynamic_slice(pattern[0].astype(jnp.float32) * a0[:, None] * a0[None, :], *here)
    mask1 = lax.dynamic_slice(pattern[1].astype(jnp.float32) * a1[:, None] * a1[None, :], *here)
    kept = lax.dynamic_slice(a1[:, None] * a1[None, :], *here)

    mask_c = lax.dynamic_slice(
        pattern[0].astype(jnp.float32) * a0[:, None] * a0[None, :],
        (row_first, q1 * PB),
        (rb, PB),
    )
    mask_r = lax.dynamic_slice(
        pattern[0].astype(jnp.float32) * a0[:, None] * a0[None, :],
        (q1 * PB, col_first),
        (PB, cb),
    )

    panel0 = jnp.where(col == q0, matrix, 0.0)
    panel1 = jnp.where(col == q1, matrix, 0.0)
    panel0, panel1, matrix, listed = lax.optimization_barrier((panel0, panel1, matrix, lists[0]))
    left0, column1 = lax.psum((panel0, panel1), "col")
    mine = lax.dynamic_slice(listed, *here)

    candidates = jnp.stack(
        [
            lax.dynamic_slice_in_dim(matrix, (q0 & 1) * half, half, 0),
            lax.dynamic_slice_in_dim(matrix, (q1 & 1) * half, half, 0),
        ]
    )
    part0, part1, inverse_part, mine = lax.optimization_barrier(
        (*exchange_row(candidates, row, (q0 >> 1, q1 >> 1)), inverses[0], mine)
    )
    theirs = xor_send(mine, "layer", 2)
    rows01 = jnp.concatenate(gather_row(jnp.stack([part0, part1]), row), axis=1)
    inv = jnp.concatenate(gather_row(inverse_part, row), axis=1)
    x_part = spread_part(part0, col, q1)
    y_part = spread_part(part1, col, q0)
    crossed = jnp.concatenate(gather_row(jnp.stack([x_part, y_part]), row), axis=1)
    listed = lax.all_gather(mine, "layer", axis_index_groups=Y_GROUPS)

    right0 = matmul(inv[0], rows01[0])
    right0x = matmul(inv[0], crossed[0])
    right1 = matmul(inv[1], rows01[1] - by_blocks(matmul(crossed[1], right0), mask_r))
    def bit(values, b):
        return values // 2**b % 2

    taken = bit(mine, 0).reshape(-1)
    plan = plan_exchange(bit(mine, 1) * kept > 0, bit(theirs, 1) * kept > 0)
    right0, right0x, right1, listed, taken, plan, left0, column1 = lax.optimization_barrier(
        (right0, right0x, right1, listed, taken, plan, left0, column1)
    )

    left1 = column1 - by_blocks(matmul(left0, right0x), mask_c)
    matrix = matrix - by_blocks(matmul(left0, right0), mask0)
    acc = by_blocks(matrix - by_blocks(matmul(left1, right1), mask1), kept)

    acc = listed_exchange(acc, xor_send(acc, "layer", 1), taken, plan, 2)

    yy = layer // 4
    qb = rb // 4

    def turn(value):
        return lax.all_to_all(
            value.reshape(4, -1, cols), "layer", 0, 0, axis_index_groups=Y_GROUPS, tiled=True
        )

    held = turn(acc)
    held = [held[k] for k in range(4)]
    w = lax.dynamic_slice_in_dim(listed, yy * qb, qb, 1)
    for b in (2, 3):
        d = b - 1
        held = [held[k] + by_blocks(held[k ^ d], bit(w[k], b).astype(jnp.float32)) for k in range(4)]
    return turn(jnp.stack(held)).reshape(1, rows, cols)


def solution(mesh):
    placed = (
        P("layer", "row", "col"),
        P("layer", None, "row", None),
        P(),
        P(),
        P("layer", None, None),
    )
    return jax.shard_map(
        body, mesh=mesh, in_specs=placed, out_specs=P("layer", "row", "col"), check_vma=False
    )
```
